128 devices in a mesh: dp: 8 (over z, core), expert: 16 (over y, x).
Axes of the slice: x: 4, y: 4, z: 4, core: 2. Of those that a mesh axis runs over, the one named last changes fastest.
Arguments:
- tokens: bfloat16 [16384, 4096], P(('dp', 'expert')), may hold values from -6 to 6
- routes: int32 [16384, 2], P(('dp', 'expert')), may hold values from 0 to 15, all different within a row; in each aligned block of 128 rows (0 to 127, 128 to 255, ...) at most 24 rows name the same one
- gates: float32 [16384, 2], P(('dp', 'expert')), may hold values from 0.1 to 1
- cotangent: bfloat16 [16384, 4096], P(('dp', 'expert')), may hold values from -6 to 6
- w_gate: bfloat16 [16, 4096, 768], P('expert'), may hold values from -0.09375 to 0.09375
- w_up: bfloat16 [16, 4096, 768], P('expert'), may hold values from -0.09375 to 0.09375
- w_down: bfloat16 [16, 768, 4096], P('expert'), may hold values from -0.21875 to 0.21875
Outputs:
- mixed: bfloat16 [16384, 4096], P(('dp', 'expert'))
- grad_tokens: bfloat16 [16384, 4096], P(('dp', 'expert'))
- grad_gates: float32 [16384, 2], P(('dp', 'expert'))
- grad_w_gate: bfloat16 [16, 4096, 768], P('expert', 'dp')
- grad_w_up: bfloat16 [16, 4096, 768], P('expert', 'dp')
- grad_w_down: bfloat16 [16, 768, 4096], P('expert', 'dp')
The draws below stay inside these ranges and needn't reach their ends.
Inputs may be any that keep to these rules, and one draw needn't show every extreme that they name: `routes`: each token names 2 different experts; in the 128 rows of one device no expert is named more than 24 times, a bound that some block reaches.
All inputs are finite; a program needn't handle non-finite values.
Results may differ from the reference program's by a relative error of at most 0.017.
Values may be sent and summed in bfloat16 or wider, within the bound.
A program may use at most 128 MiB of HBM per device.

```python
import math
import jax
import jax.numpy as jnp
import numpy as np
from jax import lax

D = 4096
FF = 768
TOP = 2
TOK_DEV = 128
EXPERTS = 16
CAP_SRC = 24
TOKENS = 16384
N_DP = 8
N_EXPERT = 16


def levels(rng, dims, cuts, least, top_value):
    gain, own = 1.0, jax.random.fold_in(rng, 6)
    for dim, shards_of in cuts:
        steps = jnp.exp(jax.random.uniform(jax.random.fold_in(own, dim), (shards_of,), jnp.float32, least / len(cuts), top_value / len(cuts)))
        gain = gain * jnp.repeat(steps, dims[dim] // shards_of).reshape([-1 if axis == dim else 1 for axis in range(len(dims))])
    return gain


def deal_out(stream_key, own, number, rows, number_of, top, bound, slope):
    ranking = jax.random.permutation(stream_key, number_of)
    heavy_load, common = portions_of(number_of, rows * top, bound, slope, True), portions_of(number_of, rows * top, bound, slope, False)
    places = jnp.arange(number_of)

    def named(tallies, rotation):
        used = int((tallies > 0).sum())
        fixed = max(1, used // 4)
        passed = fixed + (places - fixed + rotation * (used - fixed)) % max(1, number_of - fixed)
        return jnp.zeros((number_of,), jnp.int32).at[ranking[jnp.where(places < fixed, places, passed)]].set(jnp.asarray(tallies, jnp.int32))

    tallies = jnp.where(number % 4 == 0, named(heavy_load, number // 4), named(common, number - number // 4 - 1))
    mixed = jax.random.permutation(jax.random.fold_in(own, 3), number_of)
    giver, receiver = mixed[0:number_of // 2 * 2:2], mixed[1:number_of // 2 * 2:2]
    slack = jnp.minimum(tallies[giver] - 1, bound - tallies[receiver]) // 2
    slack = jnp.where((giver == ranking[0]) | (receiver == ranking[0]) | (tallies[receiver] == 0), 0, jnp.maximum(slack, 0))
    passed = jax.random.randint(jax.random.fold_in(own, 4), (number_of // 2,), 0, 1 << 20) % (slack + 1)
    tallies = tallies.at[giver].add(-passed).at[receiver].add(passed)
    members = jnp.searchsorted(jnp.cumsum(tallies), jnp.arange(rows * top), side="right").astype(jnp.int32)
    listing = members.reshape(top, rows).T
    listing = listing[jax.random.permutation(jax.random.fold_in(own, 1), rows)]
    rotation = jax.random.randint(jax.random.fold_in(own, 2), (rows, 1), 0, top)
    return jnp.take_along_axis(listing, (jnp.arange(top)[None, :] + rotation) % top, axis=1)


def portions_of(amount, total, reach, lean, full):
    weights = [(1 << 20) // math.isqrt(rank ** lean) + 1 for rank in range(1, amount + 1)]
    largest = reach if full else min(reach, max(-(-total // amount), total * weights[0] // sum(weights)))
    least = 1 if total - largest >= amount - 1 else 0
    holding, rest = [largest] + [least] * (amount - 1), total - largest - least * (amount - 1)
    while rest > 0:
        candidates = [i for i in range(1, amount) if holding[i] < largest] or [i for i in range(1, amount) if holding[i] < reach]
        pool, budget = sum([weights[i] for i in candidates]), rest
        for i in candidates:
            addition = min(reach - holding[i], max(1, budget * weights[i] // pool), rest)
            holding[i] = holding[i] + addition
            rest = rest - addition
    return np.array(holding)


def normal_values(stream_key, shape, spread, limit, pieces=(), held_as=jnp.bfloat16):
    drawn = spread * jax.random.normal(stream_key, shape, jnp.float32)
    if pieces:
        drawn = drawn * levels(stream_key, shape, pieces, -0.22, 0.18)
    return jnp.clip(drawn, -limit, limit).astype(held_as)


def setup_inputs(seed: int = 0) -> dict:
    splits = jax.random.split(jax.random.key(seed), 8)
    tokens = normal_values(splits[0], (TOKENS, D), 1.0, 6.0, ((0, 128),))
    routes_keys = jax.random.split(jax.random.fold_in(splits[1], 1), TOKENS // TOK_DEV)
    routes_turns = jax.random.permutation(jax.random.fold_in(splits[1], 3), TOKENS // TOK_DEV)
    routes = jax.vmap(lambda own, number: deal_out(jax.random.fold_in(splits[1], 2), own, number, TOK_DEV, EXPERTS, TOP, CAP_SRC, 2))(routes_keys, routes_turns).reshape((TOKENS, TOP))
    gates = jnp.clip(jnp.exp(math.log(1.0) - 2.3025851 * jax.random.uniform(splits[2], (TOKENS, TOP), jnp.float32) ** levels(splits[2], (TOKENS, TOP), ((0, 128),), -0.2, 0.2)), 0.1, 1.0)
    cotangent = normal_values(splits[3], (TOKENS, D), 1.0, 6.0, ((0, 128),))
    w_gate = normal_values(splits[4], (EXPERTS, D, FF), D ** -0.5, 0.09375, ((0, 16),))
    w_up = normal_values(splits[5], (EXPERTS, D, FF), D ** -0.5, 0.09375, ((0, 16),))
    w_down = normal_values(splits[6], (EXPERTS, FF, D), FF ** -0.5, 0.21875, ((0, 16),))
    return {"tokens": tokens, "routes": routes, "gates": gates, "cotangent": cotangent, "w_gate": w_gate, "w_up": w_up, "w_down": w_down}


def slot_select(route_block):
    flat = route_block.reshape(-1)
    onehot = (flat[:, None] == jnp.arange(EXPERTS, dtype=jnp.int32)[None, :]).astype(jnp.int32)
    before = jnp.cumsum(onehot, axis=0) - onehot
    position = jnp.sum(before * onehot, axis=1)
    target = (flat * CAP_SRC + position).reshape(TOK_DEV, TOP)
    slots = jnp.arange(EXPERTS * CAP_SRC, dtype=jnp.int32)
    return (target.T[:, None, :] == slots[None, :, None]).astype(jnp.float32)


def expert_rows(rows_x, rows_d, wg, wu, wd):
    h = jnp.dot(rows_x, wg, preferred_element_type=jnp.float32)
    u = jnp.dot(rows_x, wu, preferred_element_type=jnp.float32)
    sg = jax.nn.sigmoid(h)
    act = (h * sg * u).astype(jnp.bfloat16)
    rows_out = jnp.dot(act, wd, preferred_element_type=jnp.float32).astype(jnp.bfloat16)
    da = jnp.dot(rows_d, wd.T, preferred_element_type=jnp.float32)
    dh = (da * u * sg * (1.0 + h * (1.0 - sg))).astype(jnp.bfloat16)
    du = (da * h * sg).astype(jnp.bfloat16)
    rows_dx = (jnp.dot(dh, wg.T, preferred_element_type=jnp.float32)
               + jnp.dot(du, wu.T, preferred_element_type=jnp.float32)).astype(jnp.bfloat16)
    return rows_out, rows_dx, act, dh, du


def rounded(value):
    return lax.optimization_barrier(value.astype(jnp.bfloat16)).astype(jnp.float32)


def reference(tokens, routes, gates, cotangent, w_gate, w_up, w_down):
    blocks = N_DP * N_EXPERT
    slot_rows = EXPERTS * CAP_SRC
    select = jax.vmap(slot_select)(routes.reshape(blocks, TOK_DEV, TOP))
    tok_blocks = tokens.reshape(blocks, TOK_DEV, D).astype(jnp.float32)
    gate_blocks = gates.reshape(blocks, TOK_DEV, TOP)
    cot_blocks = cotangent.reshape(blocks, TOK_DEV, D).astype(jnp.float32)
    xbuf = jnp.einsum("bkrt,btd->brd", select, tok_blocks).astype(jnp.bfloat16)
    dpair = (gate_blocks[:, :, :, None] * cot_blocks[:, :, None, :]).astype(jnp.bfloat16)
    dbuf = jnp.einsum("bkrt,btkd->brd", select, dpair.astype(jnp.float32)).astype(jnp.bfloat16)

    def to_experts(buf):
        buf = buf.reshape(N_DP, N_EXPERT, EXPERTS, CAP_SRC, D).transpose(2, 0, 1, 3, 4)
        return buf.reshape(EXPERTS, N_DP, N_EXPERT * CAP_SRC, D)

    def one_expert(items):
        xe, de, wg, wu, wd = items

        def replica(carry, pair):
            rows_x, rows_d = pair
            rows_out, rows_dx, act, dh, du = expert_rows(rows_x, rows_d, wg, wu, wd)
            sum_g = carry[0] + rounded(jnp.dot(rows_x.T, dh, preferred_element_type=jnp.float32))
            sum_u = carry[1] + rounded(jnp.dot(rows_x.T, du, preferred_element_type=jnp.float32))
            sum_d = carry[2] + rounded(jnp.dot(act.T, rows_d, preferred_element_type=jnp.float32))
            return (sum_g, sum_u, sum_d), (rows_out, rows_dx)

        init = (jnp.zeros((D, FF), jnp.float32), jnp.zeros((D, FF), jnp.float32), jnp.zeros((FF, D), jnp.float32))
        sums, outs = lax.scan(replica, init, (xe, de))
        return outs[0], outs[1], sums[0].astype(jnp.bfloat16), sums[1].astype(jnp.bfloat16), sums[2].astype(jnp.bfloat16)

    outs, dxs, grad_g, grad_u, grad_d = lax.map(one_expert, (to_experts(xbuf), to_experts(dbuf), w_gate, w_up, w_down))

    def to_blocks(buf):
        buf = buf.reshape(EXPERTS, N_DP, N_EXPERT, CAP_SRC, D).transpose(1, 2, 0, 3, 4)
        return buf.reshape(blocks, slot_rows, D).astype(jnp.float32)

    out_pair = jnp.einsum("bkrt,brd->btkd", select, to_blocks(outs))
    mixed = jnp.sum(gate_blocks[:, :, :, None] * out_pair, axis=2).astype(jnp.bfloat16)
    grad_gates = jnp.sum(cot_blocks[:, :, None, :] * out_pair, axis=3)
    grad_tokens = jnp.einsum("bkrt,brd->btd", select, to_blocks(dxs)).astype(jnp.bfloat16)
    return (mixed.reshape(TOKENS, D), grad_tokens.reshape(TOKENS, D), grad_gates.reshape(TOKENS, TOP),
            grad_g, grad_u, grad_d)
```

```python
import jax
import jax.numpy as jnp
from jax import lax
from jax.experimental import pallas as pl
from jax.experimental.pallas import tpu as pltpu
from jax.sharding import PartitionSpec as P

MESH = pl.DeviceIdType.MESH
F32, BF16 = jnp.float32, jnp.bfloat16
SIDE = 4
GROUPS = (
    ((2, 1), (2, 3), (0, 1), (0, 3)),
    ((1, 2), (3, 2), (1, 0), (3, 0)),
    ((2, 2),),
    ((0, 2), (2, 0)),
    ((1, 1), (3, 3)),
    ((1, 3), (3, 1)),
)
SHIFTS = tuple(shift for group in GROUPS for shift in group)
X, DY, OUT, DX = range(4)


def nn(a, b):
    return lax.dot_general(a, b, (((1,), (0,)), ((), ())), preferred_element_type=F32)


def nt(a, b):
    return lax.dot_general(a, b, (((1,), (1,)), ((), ())), preferred_element_type=F32)


def tn(a, b):
    return lax.dot_general(a, b, (((0,), (0,)), ((), ())), preferred_element_type=F32)


def kernel(
    routes, gates, tok_in, cot_in, wg_in, wu_in, wd_in,
    mixed, grad_tok, grad_gates, grad_g, grad_u, grad_d, out_back,
    tok, cot, wg, wu, wd, sel, sel_t, buf_a, buf_b, xr, dd, xs, h, u, act, dhc, duc, act_t, act_s, dwg, dwu,
    zr_g, zr_u, zr_d, gg,
    send, recv, local, sib_send, sib_recv, z_send, z_recv, load, store, credit,
):
    n_exp, cap, model = buf_a.shape
    rows = n_exp * cap
    hidden = act.shape[1]
    toks = tok.shape[0]
    r, e = lax.axis_index("dp"), lax.axis_index("expert")
    z, c = r // 2, r % 2
    y, x = e // SIDE, e % SIDE

    def peer(shift, sign=1):
        dy, dx = shift
        return (y + sign * dy + SIDE) % SIDE * SIDE + (x + sign * dx + SIDE) % SIDE

    sibling = (r + 1 - 2 * c, e)
    z_up, z_down, z_far = (z + 1) % SIDE, (z + 3) % SIDE, (z + 2) % SIDE
    up, down = (z_up * 2 + c, e), (z_down * 2 + c, e)

    loads = [
        pltpu.make_async_copy(src, dst, load.at[i])
        for i, (src, dst) in enumerate(((tok_in, tok), (cot_in, cot), (wg_in.at[0], wg), (wu_in.at[0], wu), (wd_in.at[0], wd)))
    ]
    for copy in loads:
        copy.start()
    barrier = pltpu.get_barrier_semaphore()
    for shift in SHIFTS:
        pl.semaphore_signal(barrier, inc=1, device_id=(r, peer(shift)), device_id_type=MESH)
    for device in (sibling, up, down):
        pl.semaphore_signal(barrier, inc=1, device_id=device, device_id_type=MESH)

    r0, r1 = routes[0:1, :], routes[1:2, :]
    g0, g1 = gates[0:1, :], gates[1:2, :]
    expert_id = lax.broadcasted_iota(jnp.int32, (n_exp, toks), 0)
    on0, on1 = expert_id == r0, expert_id == r1
    named = jnp.where(on0 | on1, 1.0, 0.0).astype(BF16)
    before = lax.broadcasted_iota(jnp.int32, (toks, toks), 0) < lax.broadcasted_iota(jnp.int32, (toks, toks), 1)
    place = nn(named, jnp.where(before, 1.0, 0.0).astype(BF16))
    s0 = jnp.sum(jnp.where(on0, place, 0.0), axis=0, keepdims=True) + (r0 * cap).astype(F32)
    s1 = jnp.sum(jnp.where(on1, place, 0.0), axis=0, keepdims=True) + (r1 * cap).astype(F32)
    slot = lax.broadcasted_iota(jnp.int32, (rows, toks), 0).astype(F32)
    hit0, hit1 = slot == s0, slot == s1
    sel[...] = jnp.where(hit0 | hit1, 1.0, 0.0).astype(BF16)
    row_gate = jnp.sum(jnp.where(hit0, g0, 0.0) + jnp.where(hit1, g1, 0.0), axis=1, keepdims=True)
    line = lax.broadcasted_iota(jnp.int32, (toks, toks), 0)
    columns = jnp.where(line == 0, s0, jnp.where(line == 1, s1, jnp.where(line == 2, g0, g1))).T
    slot_t = lax.broadcasted_iota(jnp.int32, (toks, rows), 1).astype(F32)
    sel_t[0:toks, :] = jnp.where(slot_t == columns[:, 0:1], 1.0, 0.0).astype(BF16)
    sel_t[toks : 2 * toks, :] = jnp.where(slot_t == columns[:, 1:2], 1.0, 0.0).astype(BF16)
    gate0, gate1 = columns[:, 2:3], columns[:, 3:4]

    def chunks(total, size, body):
        @pl.loop(0, total // size)
        def _(i):
            body(i, pl.ds(pl.multiple_of(i * size, size), size))

    source = (buf_a, buf_b, buf_a, buf_b)
    target = (xr, dd, out_back, xr)

    def block(kind, i):
        to = peer(SHIFTS[i])
        return pltpu.make_async_remote_copy(
            src_ref=source[kind].at[to], dst_ref=target[kind].at[e],
            send_sem=send.at[kind, i], recv_sem=recv.at[kind, i],
            device_id=(r, to), device_id_type=MESH,
        )

    def arriving(kind, i):
        return pltpu.make_async_remote_copy(
            src_ref=source[kind].at[e], dst_ref=target[kind].at[peer(SHIFTS[i], -1)],
            send_sem=send.at[kind, i], recv_sem=recv.at[kind, i],
            device_id=(r, peer(SHIFTS[i])), device_id_type=MESH,
        )

    def own(kind):
        return pltpu.make_async_copy(source[kind].at[e], target[kind].at[e], local.at[kind])

    def begin(kind, after=None):
        own(kind).start()
        first = 0
        for group in GROUPS:
            for i in range(first, first + len(group)):
                if after is not None:
                    block(after, i).wait_send()
            for i in range(first, first + len(group)):
                block(kind, i).start()
            first += len(group)

    def finish(kind):
        own(kind).wait()
        for i in range(len(SHIFTS)):
            arriving(kind, i).wait_recv()

    loads[0].wait()

    def fill_x(_, at):
        buf_a[:, :, at] = nn(sel[...], tok[:, at]).astype(BF16).reshape(n_exp, cap, at.size)

    chunks(model, 1024, fill_x)
    pl.semaphore_wait(barrier, len(SHIFTS) + 3)
    begin(X)
    loads[1].wait()

    def fill_d(_, at):
        buf_b[:, :, at] = (nn(sel[...], cot[:, at]) * row_gate).astype(BF16).reshape(n_exp, cap, at.size)

    chunks(model, 1024, fill_d)
    begin(DY, after=X)

    finish(X)
    part = model // (2 * SIDE)

    def x_part(zz, core):
        return pl.ds(pl.multiple_of((zz * 2 + core) * part, part), part)

    def to_sibling(src, dst, i):
        return pltpu.make_async_remote_copy(
            src_ref=src, dst_ref=dst, send_sem=sib_send.at[i], recv_sem=sib_recv.at[i],
            device_id=sibling, device_id_type=MESH,
        )

    sib_x = [to_sibling(xr.at[:, :, x_part(zz, 1 - c)], xs.at[zz], zz) for zz in range(SIDE)]
    for copy in sib_x:
        copy.start()
    loads[2].wait()
    loads[3].wait()

    def up_proj(_, at):
        full = xr[...].reshape(rows, model)
        hv = nn(full, wg[:, at])
        uv = nn(full, wu[:, at])
        h[:, at] = hv
        u[:, at] = uv
        act[:, at] = (hv * jax.nn.sigmoid(hv) * uv).astype(BF16)

    chunks(hidden, 256, up_proj)
    fslice = hidden // (2 * SIDE)
    for half in range(2):
        piece = act[:, half * SIDE * fslice : (half + 1) * SIDE * fslice].astype(F32).T.astype(BF16)
        for q in range(SIDE):
            index = half * SIDE + q
            act_t[index % 2, index // 2] = piece[q * fslice : (q + 1) * fslice, :]
    sib_act = to_sibling(act_t.at[1 - c], act_s, 4)
    sib_act.start()
    loads[4].wait()

    def down_proj(_, at):
        buf_a[:, :, at] = nn(act[...], wd[:, at]).astype(BF16).reshape(n_exp, cap, at.size)

    chunks(model, 1024, down_proj)
    begin(OUT, after=DY)

    finish(DY)
    sib_d = to_sibling(dd.at[pl.ds(0, n_exp)], dd.at[pl.ds(n_exp, n_exp)], 5)
    sib_d.start()

    def back_act(_, at):
        da = nt(dd[0:n_exp].reshape(rows, model), wd[at, :])
        hv, uv = h[:, at], u[:, at]
        sg = jax.nn.sigmoid(hv)
        dhc[0:rows, at] = (da * uv * sg * (1.0 + hv * (1.0 - sg))).astype(BF16)
        duc[0:rows, at] = (da * hv * sg).astype(BF16)

    chunks(hidden, 256, back_act)
    sib_dh = to_sibling(dhc.at[pl.ds(0, rows)], dhc.at[pl.ds(rows, rows)], 6)
    sib_du = to_sibling(duc.at[pl.ds(0, rows)], duc.at[pl.ds(rows, rows)], 7)
    sib_dh.start()
    sib_du.start()

    sib_act.wait()
    sib_d.wait()

    def grad_down(_, at):
        left = jnp.concatenate([act_t[c].reshape(SIDE * fslice, rows), act_s[...].reshape(SIDE * fslice, rows)], axis=1)
        wd[0 : SIDE * fslice, at] = nn(left, dd[:, :, at].reshape(2 * rows, at.size)).astype(BF16)

    chunks(model, 512, grad_down)

    half_f, half_p = fslice // 2, part // 2

    def half_of(kind, zz, half):
        if kind == 0:
            return wd.at[pl.ds(pl.multiple_of(zz * fslice + half * half_f, half_f), half_f)]
        return (dwg, dwu)[kind - 1].at[zz, pl.ds(half * half_p, half_p)]

    zr = (zr_d, zr_g, zr_u)

    def hop(kind, i, src, device):
        return pltpu.make_async_remote_copy(
            src_ref=src, dst_ref=zr[kind].at[i], send_sem=z_send.at[kind, i], recv_sem=z_recv.at[kind, i],
            device_id=device, device_id_type=MESH,
        )

    def ring(kind, i):
        zz, half = ((z_far, 1), (z_far, 0), (z_up, 0), (z_down, 1), (z_up, 1), (z_down, 0))[i]
        return hop(kind, i, half_of(kind, zz, half), down if i % 2 else up)

    def first_hops(kind):
        for i in range(4):
            ring(kind, i).start()

    def relay(kind):
        for i, zz, half in ((0, z_up, 1), (1, z_down, 0)):
            ring(kind, i).wait_recv()
            mine = half_of(kind, zz, half)
            mine[...] = (mine[...].astype(F32) + zr[kind][i].astype(F32)).astype(BF16)
            ring(kind, i + 4).start()

    def total(kind, out):
        for i in (2, 3, 4, 5):
            ring(kind, i).wait_recv()
        for half, (a, b) in enumerate(((2, 5), (3, 4))):
            mine = half_of(kind, z, half)
            mine[...] = (mine[...].astype(F32) + zr[kind][a].astype(F32) + zr[kind][b].astype(F32)).astype(BF16)
        whole = wd.at[pl.ds(pl.multiple_of(z * fslice, fslice), fslice)] if kind == 0 else (dwg, dwu)[kind - 1].at[z]
        copy = pltpu.make_async_copy(whole, out.at[0], store.at[2 + kind])
        copy.start()
        return copy

    first_hops(0)
    for copy in sib_x:
        copy.wait()

    def grad_in(right, out):
        @pl.loop(0, SIDE)
        def _(i):
            zz = (z + 2 + i) % SIDE
            left = jnp.concatenate([xr[:, :, x_part(zz, c)].reshape(rows, part), xs[zz].reshape(rows, part)], axis=0)
            out[zz] = tn(left, right[...]).astype(BF16)

    sib_dh.wait()
    grad_in(dhc, dwg)
    first_hops(1)
    sib_du.wait()
    grad_in(duc, dwu)
    first_hops(2)
    for i in range(len(SHIFTS)):
        pl.semaphore_signal(credit, inc=1, device_id=(r, peer(SHIFTS[i])), device_id_type=MESH)

    def back_rows(_, at):
        buf_b[:, :, at] = (nt(dhc[0:rows], wg[at, :]) + nt(duc[0:rows], wu[at, :])).astype(BF16).reshape(n_exp, cap, at.size)

    chunks(model, 512, back_rows)
    relay(0)
    pl.semaphore_wait(credit, len(SHIFTS))
    begin(DX, after=OUT)

    finish(OUT)
    fetch = pltpu.make_async_copy(out_back, dd.at[pl.ds(n_exp, n_exp)], load.at[5])
    fetch.start()
    fetch.wait()
    gg[...] = jnp.zeros_like(gg)

    def combine(_, at):
        pairs = nn(sel_t[...], dd[n_exp : 2 * n_exp, :, at].reshape(rows, at.size))
        p0, p1 = pairs[0:toks], pairs[toks : 2 * toks]
        tok[:, at] = (gate0 * p0 + gate1 * p1).astype(BF16)
        cv = cot[:, at].astype(F32)
        for k, pk in enumerate((p0, p1)):
            prod = cv * pk
            for j in range(0, at.size, 128):
                gg[k] += prod[:, j : j + 128]

    chunks(model, 512, combine)
    mixed_out = pltpu.make_async_copy(tok, mixed, store.at[0])
    mixed_out.start()
    grad_gates[0:1, :] = jnp.sum(gg[0].T, axis=0, keepdims=True)
    grad_gates[1:2, :] = jnp.sum(gg[1].T, axis=0, keepdims=True)
    relay(1)
    relay(2)
    down_out = total(0, grad_d)

    finish(DX)

    def combine_dx(_, at):
        both = sel_t[0:toks, :] + sel_t[toks : 2 * toks, :]
        cot[:, at] = nn(both, xr[:, :, at].reshape(rows, at.size)).astype(BF16)

    chunks(model, 512, combine_dx)
    tok_out = pltpu.make_async_copy(cot, grad_tok, store.at[1])
    tok_out.start()
    gate_out = total(1, grad_g)
    up_out = total(2, grad_u)
    for i in range(len(SHIFTS)):
        block(DX, i).wait_send()
    for kind in range(3):
        for i in range(6):
            ring(kind, i).wait_send()
    for copy in (mixed_out, tok_out, down_out, gate_out, up_out):
        copy.wait()


def per_device(tokens, routes, gates, cotangent, w_gate, w_up, w_down):
    experts, replicas = lax.axis_size("expert"), lax.axis_size("dp")
    toks, model = tokens.shape
    hidden = w_gate.shape[2]
    cap = toks * routes.shape[1] * 3 // (2 * experts)
    rows = experts * cap
    part, fslice = model // replicas, hidden // replicas
    shape = jax.ShapeDtypeStruct
    any_space, vmem = pl.BlockSpec(memory_space=pl.ANY), pl.BlockSpec(memory_space=pltpu.VMEM)
    dma = pltpu.SemaphoreType.DMA
    n = len(SHIFTS)
    outs = pl.pallas_call(
        kernel,
        out_shape=(
            shape((toks, model), BF16),
            shape((toks, model), BF16),
            shape((2, toks), F32),
            shape((1, part, hidden), BF16),
            shape((1, part, hidden), BF16),
            shape((1, fslice, model), BF16),
            shape((experts, cap, model), BF16),
        ),
        in_specs=[vmem, vmem] + [any_space] * 5,
        out_specs=(any_space, any_space, vmem) + (any_space,) * 4,
        scratch_shapes=[
            pltpu.VMEM((toks, model), BF16),
            pltpu.VMEM((toks, model), BF16),
            pltpu.VMEM((model, hidden), BF16),
            pltpu.VMEM((model, hidden), BF16),
            pltpu.VMEM((hidden, model), BF16),
            pltpu.VMEM((rows, toks), BF16),
            pltpu.VMEM((2 * toks, rows), BF16),
            pltpu.VMEM((experts, cap, model), BF16),
            pltpu.VMEM((experts, cap, model), BF16),
            pltpu.VMEM((experts, cap, model), BF16),
            pltpu.VMEM((2 * experts, cap, model), BF16),
            pltpu.VMEM((SIDE, experts, cap, part), BF16),
            pltpu.VMEM((rows, hidden), F32),
            pltpu.VMEM((rows, hidden), F32),
            pltpu.VMEM((rows, hidden), BF16),
            pltpu.VMEM((2 * rows, hidden), BF16),
            pltpu.VMEM((2 * rows, hidden), BF16),
            pltpu.VMEM((2, SIDE, fslice, rows), BF16),
            pltpu.VMEM((SIDE, fslice, rows), BF16),
            pltpu.VMEM((SIDE, part, hidden), BF16),
            pltpu.VMEM((SIDE, part, hidden), BF16),
            pltpu.VMEM((6, part // 2, hidden), BF16),
            pltpu.VMEM((6, part // 2, hidden), BF16),
            pltpu.VMEM((6, fslice // 2, model), BF16),
            pltpu.VMEM((2, toks, 128), F32),
            dma((4, n)),
            dma((4, n)),
            dma((4,)),
            dma((8,)),
            dma((8,)),
            dma((3, 6)),
            dma((3, 6)),
            dma((6,)),
            dma((5,)),
            pltpu.SemaphoreType.REGULAR,
        ],
        compiler_params=pltpu.CompilerParams(
            collective_id=0, has_side_effects=True, vmem_limit_bytes=63 << 20
        ),
        name="expert_layer",
    )(routes.T, gates.T, tokens, cotangent, w_gate, w_up, w_down)
    return (outs[0], outs[1], outs[2].T, outs[3], outs[4], outs[5])


def solution(mesh):
    rows, whole = P(("dp", "expert"), None), P("expert", None, None)
    grads = P("expert", "dp", None)
    return jax.shard_map(
        per_device,
        mesh=mesh,
        in_specs=(rows,) * 4 + (whole,) * 3,
        out_specs=(rows,) * 3 + (grads,) * 3,
        check_vma=False,
    )
```

```python
import jax
import jax.numpy as jnp
from jax import lax
from jax.experimental import pallas as pl
from jax.experimental.pallas import tpu as pltpu
from jax.sharding import PartitionSpec as P

MESH = pl.DeviceIdType.MESH
F32, BF16 = jnp.float32, jnp.bfloat16
SIDE = 4
GROUPS = (
    ((1, 3), (3, 1)),
    ((1, 1), (3, 3)),
    ((0, 2), (2, 0)),
    ((2, 2),),
    ((1, 2), (3, 2), (1, 0), (3, 0)),
    ((2, 1), (2, 3), (0, 1), (0, 3)),
)
SHIFTS = tuple(shift for group in GROUPS for shift in group)
X, DY, OUT, DX = range(4)
HALVES = 2
DOWN, GATE, UP = (0, 1), 2, 3


def nn(a, b):
    return lax.dot_general(a, b, (((1,), (0,)), ((), ())), preferred_element_type=F32)


def nt(a, b):
    return lax.dot_general(a, b, (((1,), (1,)), ((), ())), preferred_element_type=F32)


def tn(a, b):
    return lax.dot_general(a, b, (((0,), (0,)), ((), ())), preferred_element_type=F32)


def kernel(
    routes, gates, tok_in, cot_in, wg_in, wu_in, wd_in,
    mixed, grad_tok, grad_gates, grad_g, grad_u, grad_d, out_back,
    tok, cot, wg, wu, wd, sel, sel_t, buf_a, buf_b, xr, dd, xs, h, u, act, dhc, duc, act_t, act_s, dwg, dwu,
    zr_g, zr_u, zr_d, dact, gg,
    send, recv, local, sib_send, sib_recv, z_send, z_recv, load, store, credit,
):
    n_exp, cap, model = buf_a.shape
    rows = n_exp * cap
    hidden = act.shape[1]
    toks = tok.shape[0]
    r, e = lax.axis_index("dp"), lax.axis_index("expert")
    z, c = r // 2, r % 2
    y, x = e // SIDE, e % SIDE

    def peer(shift, sign=1):
        dy, dx = shift
        return (y + sign * dy + SIDE) % SIDE * SIDE + (x + sign * dx + SIDE) % SIDE

    sibling = (r + 1 - 2 * c, e)
    z_up, z_down, z_far = (z + 1) % SIDE, (z + 3) % SIDE, (z + 2) % SIDE
    up, down = (z_up * 2 + c, e), (z_down * 2 + c, e)

    loads = [
        pltpu.make_async_copy(src, dst, load.at[i])
        for i, (src, dst) in enumerate(((tok_in, tok), (cot_in, cot), (wg_in.at[0], wg), (wu_in.at[0], wu), (wd_in.at[0], wd)))
    ]
    for copy in loads[:2]:
        copy.start()
    barrier = pltpu.get_barrier_semaphore()
    for shift in SHIFTS:
        pl.semaphore_signal(barrier, inc=1, device_id=(r, peer(shift)), device_id_type=MESH)
    for device in (sibling, up, down):
        pl.semaphore_signal(barrier, inc=1, device_id=device, device_id_type=MESH)

    r0, r1 = routes[0:1, :], routes[1:2, :]
    g0, g1 = gates[0:1, :], gates[1:2, :]
    expert_id = lax.broadcasted_iota(jnp.int32, (n_exp, toks), 0)
    on0, on1 = expert_id == r0, expert_id == r1
    named = jnp.where(on0 | on1, 1.0, 0.0).astype(BF16)
    before = lax.broadcasted_iota(jnp.int32, (toks, toks), 0) < lax.broadcasted_iota(jnp.int32, (toks, toks), 1)
    place = nn(named, jnp.where(before, 1.0, 0.0).astype(BF16))
    s0 = jnp.sum(jnp.where(on0, place, 0.0), axis=0, keepdims=True) + (r0 * cap).astype(F32)
    s1 = jnp.sum(jnp.where(on1, place, 0.0), axis=0, keepdims=True) + (r1 * cap).astype(F32)
    slot = lax.broadcasted_iota(jnp.int32, (rows, toks), 0).astype(F32)
    hit0, hit1 = slot == s0, slot == s1
    sel[...] = jnp.where(hit0 | hit1, 1.0, 0.0).astype(BF16)
    row_gate = jnp.sum(jnp.where(hit0, g0, 0.0) + jnp.where(hit1, g1, 0.0), axis=1, keepdims=True)
    line = lax.broadcasted_iota(jnp.int32, (toks, toks), 0)
    columns = jnp.where(line == 0, s0, jnp.where(line == 1, s1, jnp.where(line == 2, g0, g1))).T
    slot_t = lax.broadcasted_iota(jnp.int32, (toks, rows), 1).astype(F32)
    sel_t[0:toks, :] = jnp.where(slot_t == columns[:, 0:1], 1.0, 0.0).astype(BF16)
    sel_t[toks : 2 * toks, :] = jnp.where(slot_t == columns[:, 1:2], 1.0, 0.0).astype(BF16)
    gate0, gate1 = columns[:, 2:3], columns[:, 3:4]

    def chunks(total, size, body):
        @pl.loop(0, total // size)
        def _(i):
            body(i, pl.ds(pl.multiple_of(i * size, size), size))

    source = (buf_a, buf_b, buf_a, buf_b)
    target = (xr, dd, out_back, xr)
    width = model // HALVES

    def columns_of(half):
        return pl.ds(half * width, width)

    def span(kind, half):
        return pl.ds(0, model) if kind in (OUT, DX) else columns_of(half)

    def block(kind, half, i):
        to = peer(SHIFTS[i])
        return pltpu.make_async_remote_copy(
            src_ref=source[kind].at[to, :, span(kind, half)], dst_ref=target[kind].at[e, :, span(kind, half)],
            send_sem=send.at[kind, half, i], recv_sem=recv.at[kind, half, i],
            device_id=(r, to), device_id_type=MESH,
        )

    def arriving(kind, half, i):
        return pltpu.make_async_remote_copy(
            src_ref=source[kind].at[e, :, span(kind, half)],
            dst_ref=target[kind].at[peer(SHIFTS[i], -1), :, span(kind, half)],
            send_sem=send.at[kind, half, i], recv_sem=recv.at[kind, half, i],
            device_id=(r, peer(SHIFTS[i])), device_id_type=MESH,
        )

    def own(kind, half):
        return pltpu.make_async_copy(
            source[kind].at[e, :, span(kind, half)], target[kind].at[e, :, span(kind, half)], local.at[kind, half]
        )

    def begin(kind, half, after=(), groups=range(len(GROUPS))):
        if 0 in groups:
            own(kind, half).start()
        for g in groups:
            group = GROUPS[g]
            first = sum(len(x) for x in GROUPS[:g])
            for i in range(first, first + len(group)):
                for earlier in after:
                    block(*earlier, i).wait_send()
            for i in range(first, first + len(group)):
                block(kind, half, i).start()

    def finish(kind, half):
        own(kind, half).wait()
        for i in range(len(SHIFTS)):
            arriving(kind, half, i).wait_recv()

    def half_chunks(half, size, body):
        @pl.loop(0, width // size)
        def _(i):
            body(pl.ds(pl.multiple_of(half * width + i * size, size), size))

    loads[0].wait()

    def fill_x(at):
        buf_a[:, :, at] = nn(sel[...], tok[:, at]).astype(BF16).reshape(n_exp, cap, at.size)

    half_chunks(0, 1024, fill_x)
    pl.semaphore_wait(barrier, len(SHIFTS) + 3)
    begin(X, 0)
    half_chunks(1, 1024, fill_x)
    begin(X, 1)
    for copy in loads[2:]:
        copy.start()
    loads[1].wait()

    def fill_d(at):
        buf_b[:, :, at] = (nn(sel[...], cot[:, at]) * row_gate).astype(BF16).reshape(n_exp, cap, at.size)

    half_chunks(0, 1024, fill_d)
    half_chunks(1, 1024, fill_d)
    begin(DY, 0, after=((X, 0), (X, 1)))

    finish(X, 0)
    finish(X, 1)
    part = model // (2 * SIDE)

    def x_part(zz, core):
        return pl.ds(pl.multiple_of((zz * 2 + core) * part, part), part)

    def to_sibling(src, dst, i):
        return pltpu.make_async_remote_copy(
            src_ref=src, dst_ref=dst, send_sem=sib_send.at[i], recv_sem=sib_recv.at[i],
            device_id=sibling, device_id_type=MESH,
        )

    sib_x = [to_sibling(xr.at[:, :, x_part(zz, 1 - c)], xs.at[zz], zz) for zz in range(SIDE)]
    for copy in sib_x:
        copy.start()
    loads[2].wait()
    loads[3].wait()

    def up_proj(_, at):
        full = xr[...].reshape(rows, model)
        hv = nn(full, wg[:, at])
        uv = nn(full, wu[:, at])
        h[:, at] = hv
        u[:, at] = uv
        act[:, at] = (hv * jax.nn.sigmoid(hv) * uv).astype(BF16)

    chunks(hidden, 256, up_proj)
    fslice = hidden // (2 * SIDE)
    for half in range(2):
        piece = act[:, half * SIDE * fslice : (half + 1) * SIDE * fslice].astype(F32).T.astype(BF16)
        for q in range(SIDE):
            index = half * SIDE + q
            act_t[index % 2, index // 2] = piece[q * fslice : (q + 1) * fslice, :]
    sib_act = to_sibling(act_t.at[1 - c], act_s, 4)
    sib_act.start()
    loads[4].wait()

    def down_proj(_, at):
        buf_a[:, :, at] = nn(act[...], wd[:, at]).astype(BF16).reshape(n_exp, cap, at.size)

    chunks(model, 1024, down_proj)
    begin(DY, 1, after=((DY, 0),))

    finish(DY, 0)

    def sib_d(half):
        return to_sibling(
            dd.at[pl.ds(0, n_exp), :, columns_of(half)], dd.at[pl.ds(n_exp, n_exp), :, columns_of(half)], 5 + half
        )

    sib_d(0).start()

    def back_act(half):
        def body(_, at):
            dact[:, at] = nt(dd[0:n_exp, :, half * width : (half + 1) * width].reshape(rows, width), wd[at, columns_of(half)])

        return body

    chunks(hidden, 256, back_act(0))

    def grad_down(at):
        left = jnp.concatenate([act_t[c].reshape(SIDE * fslice, rows), act_s[...].reshape(SIDE * fslice, rows)], axis=1)
        wd[0 : SIDE * fslice, at] = nn(left, dd[:, :, at].reshape(2 * rows, at.size)).astype(BF16)

    sib_act.wait()
    sib_d(0).wait()
    half_chunks(0, 512, grad_down)

    half_f, half_p = fslice // 2, part // 2

    def half_of(kind, zz, half):
        if kind in DOWN:
            return wd.at[pl.ds(pl.multiple_of(zz * fslice + half * half_f, half_f), half_f), columns_of(kind)]
        return (dwg, dwu)[kind - GATE].at[zz, pl.ds(half * half_p, half_p)]

    zr = (zr_d.at[0], zr_d.at[1], zr_g, zr_u)

    def hop(kind, i, src, device):
        return pltpu.make_async_remote_copy(
            src_ref=src, dst_ref=zr[kind].at[i], send_sem=z_send.at[kind, i], recv_sem=z_recv.at[kind, i],
            device_id=device, device_id_type=MESH,
        )

    def ring(kind, i):
        zz, half = ((z_far, 1), (z_far, 0), (z_up, 0), (z_down, 1), (z_up, 1), (z_down, 0))[i]
        return hop(kind, i, half_of(kind, zz, half), down if i % 2 else up)

    def first_hops(kind):
        for i in range(4):
            ring(kind, i).start()

    def relay(kind):
        for i, zz, half in ((0, z_up, 1), (1, z_down, 0)):
            ring(kind, i).wait_recv()
            mine = half_of(kind, zz, half)
            mine[...] = (mine[...].astype(F32) + zr[kind][i].astype(F32)).astype(BF16)
            ring(kind, i + 4).start()

    def total(kind, out):
        for i in (2, 3, 4, 5):
            ring(kind, i).wait_recv()
        for half, (a, b) in enumerate(((2, 5), (3, 4))):
            mine = half_of(kind, z, half)
            mine[...] = (mine[...].astype(F32) + zr[kind][a].astype(F32) + zr[kind][b].astype(F32)).astype(BF16)
        if kind in DOWN:
            whole = wd.at[pl.ds(pl.multiple_of(z * fslice, fslice), fslice), columns_of(kind)]
            out = out.at[0, :, columns_of(kind)]
        else:
            whole, out = (dwg, dwu)[kind - GATE].at[z], out.at[0]
        copy = pltpu.make_async_copy(whole, out, store.at[2 + kind])
        copy.start()
        return copy

    first_hops(DOWN[0])
    begin(OUT, 0, after=((DY, 1),))
    relay(DOWN[0])
    finish(DY, 1)
    sib_d(1).start()

    def back_act_last(_, at):
        da = dact[:, at] + nt(dd[0:n_exp, :, width:].reshape(rows, width), wd[at, columns_of(1)])
        hv, uv = h[:, at], u[:, at]
        sg = jax.nn.sigmoid(hv)
        dhc[0:rows, at] = (da * uv * sg * (1.0 + hv * (1.0 - sg))).astype(BF16)
        duc[0:rows, at] = (da * hv * sg).astype(BF16)

    chunks(hidden, 256, back_act_last)
    sib_dh = to_sibling(dhc.at[pl.ds(0, rows)], dhc.at[pl.ds(rows, rows)], 7)
    sib_du = to_sibling(duc.at[pl.ds(0, rows)], duc.at[pl.ds(rows, rows)], 8)
    sib_dh.start()
    sib_du.start()
    sib_d(1).wait()
    half_chunks(1, 512, grad_down)
    first_hops(DOWN[1])
    for copy in sib_x:
        copy.wait()

    def grad_in(right, out):
        @pl.loop(0, SIDE)
        def _(i):
            zz = (z + 2 + i) % SIDE
            left = jnp.concatenate([xr[:, :, x_part(zz, c)].reshape(rows, part), xs[zz].reshape(rows, part)], axis=0)
            out[zz] = tn(left, right[...]).astype(BF16)

    sib_dh.wait()
    grad_in(dhc, dwg)
    first_hops(GATE)
    sib_du.wait()
    grad_in(duc, dwu)
    first_hops(UP)
    for i in range(len(SHIFTS)):
        pl.semaphore_signal(credit, inc=1, device_id=(r, peer(SHIFTS[i])), device_id_type=MESH)

    def back_rows(_, at):
        buf_b[:, :, at] = (nt(dhc[0:rows], wg[at, :]) + nt(duc[0:rows], wu[at, :])).astype(BF16).reshape(n_exp, cap, at.size)

    chunks(model, 512, back_rows)
    relay(DOWN[1])
    pl.semaphore_wait(credit, len(SHIFTS))
    begin(DX, 0, after=((OUT, 0),))

    finish(OUT, 0)
    fetch = pltpu.make_async_copy(out_back, dd.at[pl.ds(n_exp, n_exp)], load.at[5])
    fetch.start()
    fetch.wait()
    gg[...] = jnp.zeros_like(gg)

    def combine(_, at):
        pairs = nn(sel_t[...], dd[n_exp : 2 * n_exp, :, at].reshape(rows, at.size))
        p0, p1 = pairs[0:toks], pairs[toks : 2 * toks]
        tok[:, at] = (gate0 * p0 + gate1 * p1).astype(BF16)
        cv = cot[:, at].astype(F32)
        for k, pk in enumerate((p0, p1)):
            prod = cv * pk
            for j in range(0, at.size, 128):
                gg[k] += prod[:, j : j + 128]

    chunks(model, 512, combine)
    mixed_out = pltpu.make_async_copy(tok, mixed, store.at[0])
    mixed_out.start()
    grad_gates[0:1, :] = jnp.sum(gg[0].T, axis=0, keepdims=True)
    grad_gates[1:2, :] = jnp.sum(gg[1].T, axis=0, keepdims=True)
    relay(GATE)
    relay(UP)
    stores = [mixed_out] + [total(kind, grad_d) for kind in DOWN]

    def combine_dx(at):
        both = sel_t[0:toks, :] + sel_t[toks : 2 * toks, :]
        cot[:, at] = nn(both, xr[:, :, at].reshape(rows, at.size)).astype(BF16)

    finish(DX, 0)
    chunks(model, 512, lambda _, at: combine_dx(at))
    stores.append(pltpu.make_async_copy(cot, grad_tok, store.at[1]))
    stores[-1].start()
    stores += [total(GATE, grad_g), total(UP, grad_u)]
    for i in range(len(SHIFTS)):
        block(DX, 0, i).wait_send()
    for kind in (*DOWN, GATE, UP):
        for i in range(6):
            ring(kind, i).wait_send()
    for copy in stores:
        copy.wait()


def copy_out(*refs):
    n = len(refs) // 3
    ins, outs, held, (load, store) = refs[:n], refs[n : 2 * n], refs[2 * n : 3 * n], refs[3 * n :]
    loads = [pltpu.make_async_copy(ins[i], held[i], load.at[i]) for i in range(n)]
    stores = [pltpu.make_async_copy(held[i], outs[i], store.at[i]) for i in range(n)]
    for copy in loads:
        copy.start()
    for first, second in zip(loads, stores):
        first.wait()
        second.start()
    for copy in stores:
        copy.wait()


def per_device(tokens, routes, gates, cotangent, w_gate, w_up, w_down):
    experts, replicas = lax.axis_size("expert"), lax.axis_size("dp")
    toks, model = tokens.shape
    hidden = w_gate.shape[2]
    cap = toks * routes.shape[1] * 3 // (2 * experts)
    rows = experts * cap
    part, fslice = model // replicas, hidden // replicas
    shape = jax.ShapeDtypeStruct
    any_space, vmem = pl.BlockSpec(memory_space=pl.ANY), pl.BlockSpec(memory_space=pltpu.VMEM)
    dma = pltpu.SemaphoreType.DMA
    n = len(SHIFTS)
    outs = pl.pallas_call(
        kernel,
        out_shape=(
            shape((toks, model), BF16),
            shape((toks, model), BF16),
            shape((2, toks), F32),
            shape((1, part, hidden), BF16),
            shape((1, part, hidden), BF16),
            shape((1, fslice, model), BF16),
            shape((experts, cap, model), BF16),
        ),
        in_specs=[vmem, vmem] + [any_space] * 5,
        out_specs=(any_space, any_space, vmem) + (any_space,) * 4,
        scratch_shapes=[
            pltpu.VMEM((toks, model), BF16),
            pltpu.VMEM((toks, model), BF16),
            pltpu.VMEM((model, hidden), BF16),
            pltpu.VMEM((model, hidden), BF16),
            pltpu.VMEM((hidden, model), BF16),
            pltpu.VMEM((rows, toks), BF16),
            pltpu.VMEM((2 * toks, rows), BF16),
            pltpu.VMEM((experts, cap, model), BF16),
            pltpu.VMEM((experts, cap, model), BF16),
            pltpu.VMEM((experts, cap, model), BF16),
            pltpu.VMEM((2 * experts, cap, model), BF16),
            pltpu.VMEM((SIDE, experts, cap, part), BF16),
            pltpu.VMEM((rows, hidden), F32),
            pltpu.VMEM((rows, hidden), F32),
            pltpu.VMEM((rows, hidden), BF16),
            pltpu.VMEM((2 * rows, hidden), BF16),
            pltpu.VMEM((2 * rows, hidden), BF16),
            pltpu.VMEM((2, SIDE, fslice, rows), BF16),
            pltpu.VMEM((SIDE, fslice, rows), BF16),
            pltpu.VMEM((SIDE, part, hidden), BF16),
            pltpu.VMEM((SIDE, part, hidden), BF16),
            pltpu.VMEM((6, part // 2, hidden), BF16),
            pltpu.VMEM((6, part // 2, hidden), BF16),
            pltpu.VMEM((2, 6, fslice // 2, model // 2), BF16),
            pltpu.VMEM((rows, hidden), F32),
            pltpu.VMEM((2, toks, 128), F32),
            dma((4, HALVES, n)),
            dma((4, HALVES, n)),
            dma((4, HALVES)),
            dma((9,)),
            dma((9,)),
            dma((4, 6)),
            dma((4, 6)),
            dma((6,)),
            dma((6,)),
            pltpu.SemaphoreType.REGULAR,
        ],
        compiler_params=pltpu.CompilerParams(
            collective_id=0, has_side_effects=True, vmem_limit_bytes=63 << 20
        ),
        name="expert_layer",
    )(routes.T, gates.T, tokens, cotangent, w_gate, w_up, w_down)
    outs = outs[:6]
    outs = pl.pallas_call(
        copy_out,
        out_shape=tuple(shape(o.shape, o.dtype) for o in outs),
        in_specs=[any_space] * len(outs),
        out_specs=(any_space,) * len(outs),
        scratch_shapes=[pltpu.VMEM(o.shape, o.dtype) for o in outs] + [dma((len(outs),))] * 2,
        compiler_params=pltpu.CompilerParams(vmem_limit_bytes=60 << 20),
        name="copy_out",
    )(*outs)
    return (outs[0], outs[1], outs[2].T, outs[3], outs[4], outs[5])


def solution(mesh):
    rows, whole = P(("dp", "expert"), None), P("expert", None, None)
    grads = P("expert", "dp", None)
    return jax.shard_map(
        per_device,
        mesh=mesh,
        in_specs=(rows,) * 4 + (whole,) * 3,
        out_specs=(rows,) * 3 + (grads,) * 3,
        check_vma=False,
    )
```

```python
import jax
import jax.numpy as jnp
from jax import lax
from jax.experimental import pallas as pl
from jax.experimental.pallas import tpu as pltpu
from jax.sharding import PartitionSpec as P

MESH = pl.DeviceIdType.MESH
F32, BF16 = jnp.float32, jnp.bfloat16
SIDE = 4
GROUPS = (
    ((1, 3), (3, 1)),
    ((1, 1), (3, 3)),
    ((0, 2), (2, 0)),
    ((2, 2),),
    ((1, 2), (3, 2), (1, 0), (3, 0)),
    ((2, 1), (2, 3), (0, 1), (0, 3)),
)
SHIFTS = tuple(shift for group in GROUPS for shift in group)
X, DY, OUT, DX = range(4)
HALVES = 2
DOWN, GATE, UP = (0, 1), 2, 3


def nn(a, b):
    return lax.dot_general(a, b, (((1,), (0,)), ((), ())), preferred_element_type=F32)


def nt(a, b):
    return lax.dot_general(a, b, (((1,), (1,)), ((), ())), preferred_element_type=F32)


def tn(a, b):
    return lax.dot_general(a, b, (((0,), (0,)), ((), ())), preferred_element_type=F32)


def kernel(
    routes, gates, tok_in, cot_in, wg_in, wu_in, wd_in,
    mixed, grad_tok, grad_gates, grad_g, grad_u, grad_d, out_back,
    tok, cot, wg, wu, wd, sel, sel_t, buf_a, buf_b, xr, dd, xs, h, u, act, dhc, duc, act_t, act_s, dwg, dwu,
    zr_g, zr_u, zr_d, dact, gg,
    send, recv, local, sib_send, sib_recv, z_send, z_recv, load, store, credit,
):
    n_exp, cap, model = buf_a.shape
    rows = n_exp * cap
    hidden = act.shape[1]
    toks = tok.shape[0]
    r, e = lax.axis_index("dp"), lax.axis_index("expert")
    z, c = r // 2, r % 2
    y, x = e // SIDE, e % SIDE

    def peer(shift, sign=1):
        dy, dx = shift
        return (y + sign * dy + SIDE) % SIDE * SIDE + (x + sign * dx + SIDE) % SIDE

    sibling = (r + 1 - 2 * c, e)
    z_up, z_down, z_far = (z + 1) % SIDE, (z + 3) % SIDE, (z + 2) % SIDE
    up, down = (z_up * 2 + c, e), (z_down * 2 + c, e)

    loads = [
        pltpu.make_async_copy(src, dst, load.at[i])
        for i, (src, dst) in enumerate(((tok_in, tok), (cot_in, cot), (wg_in.at[0], wg), (wu_in.at[0], wu), (wd_in.at[0], wd)))
    ]
    for copy in loads[:2]:
        copy.start()
    barrier = pltpu.get_barrier_semaphore()
    for shift in SHIFTS:
        pl.semaphore_signal(barrier, inc=1, device_id=(r, peer(shift)), device_id_type=MESH)
    for device in (sibling, up, down):
        pl.semaphore_signal(barrier, inc=1, device_id=device, device_id_type=MESH)

    r0, r1 = routes[0:1, :], routes[1:2, :]
    g0, g1 = gates[0:1, :], gates[1:2, :]
    expert_id = lax.broadcasted_iota(jnp.int32, (n_exp, toks), 0)
    on0, on1 = expert_id == r0, expert_id == r1
    named = jnp.where(on0 | on1, 1.0, 0.0).astype(BF16)
    before = lax.broadcasted_iota(jnp.int32, (toks, toks), 0) < lax.broadcasted_iota(jnp.int32, (toks, toks), 1)
    place = nn(named, jnp.where(before, 1.0, 0.0).astype(BF16))
    s0 = jnp.sum(jnp.where(on0, place, 0.0), axis=0, keepdims=True) + (r0 * cap).astype(F32)
    s1 = jnp.sum(jnp.where(on1, place, 0.0), axis=0, keepdims=True) + (r1 * cap).astype(F32)
    slot = lax.broadcasted_iota(jnp.int32, (rows, toks), 0).astype(F32)
    hit0, hit1 = slot == s0, slot == s1
    sel[...] = jnp.where(hit0 | hit1, 1.0, 0.0).astype(BF16)
    row_gate = jnp.sum(jnp.where(hit0, g0, 0.0) + jnp.where(hit1, g1, 0.0), axis=1, keepdims=True)
    line = lax.broadcasted_iota(jnp.int32, (toks, toks), 0)
    columns = jnp.where(line == 0, s0, jnp.where(line == 1, s1, jnp.where(line == 2, g0, g1))).T
    slot_t = lax.broadcasted_iota(jnp.int32, (toks, rows), 1).astype(F32)
    sel_t[0:toks, :] = jnp.where(slot_t == columns[:, 0:1], 1.0, 0.0).astype(BF16)
    sel_t[toks : 2 * toks, :] = jnp.where(slot_t == columns[:, 1:2], 1.0, 0.0).astype(BF16)
    gate0, gate1 = columns[:, 2:3], columns[:, 3:4]

    def chunks(total, size, body):
        @pl.loop(0, total // size)
        def _(i):
            body(i, pl.ds(pl.multiple_of(i * size, size), size))

    source = (buf_a, buf_b, buf_a, buf_b)
    target = (xr, dd, out_back, xr)
    width = model // HALVES

    def columns_of(half):
        return pl.ds(half * width, width)

    def block(kind, half, i):
        to = peer(SHIFTS[i])
        return pltpu.make_async_remote_copy(
            src_ref=source[kind].at[to, :, columns_of(half)], dst_ref=target[kind].at[e, :, columns_of(half)],
            send_sem=send.at[kind, half, i], recv_sem=recv.at[kind, half, i],
            device_id=(r, to), device_id_type=MESH,
        )

    def arriving(kind, half, i):
        return pltpu.make_async_remote_copy(
            src_ref=source[kind].at[e, :, columns_of(half)],
            dst_ref=target[kind].at[peer(SHIFTS[i], -1), :, columns_of(half)],
            send_sem=send.at[kind, half, i], recv_sem=recv.at[kind, half, i],
            device_id=(r, peer(SHIFTS[i])), device_id_type=MESH,
        )

    def own(kind, half):
        return pltpu.make_async_copy(
            source[kind].at[e, :, columns_of(half)], target[kind].at[e, :, columns_of(half)], local.at[kind, half]
        )

    def begin(kind, half, after=(), groups=range(len(GROUPS))):
        if 0 in groups:
            own(kind, half).start()
        for g in groups:
            group = GROUPS[g]
            first = sum(len(x) for x in GROUPS[:g])
            for i in range(first, first + len(group)):
                for earlier in after:
                    block(*earlier, i).wait_send()
            for i in range(first, first + len(group)):
                block(kind, half, i).start()

    def finish(kind, half):
        own(kind, half).wait()
        for i in range(len(SHIFTS)):
            arriving(kind, half, i).wait_recv()

    def half_chunks(half, size, body):
        @pl.loop(0, width // size)
        def _(i):
            body(pl.ds(pl.multiple_of(half * width + i * size, size), size))

    loads[0].wait()

    def fill_x(at):
        buf_a[:, :, at] = nn(sel[...], tok[:, at]).astype(BF16).reshape(n_exp, cap, at.size)

    half_chunks(0, 1024, fill_x)
    pl.semaphore_wait(barrier, len(SHIFTS) + 3)
    begin(X, 0)
    half_chunks(1, 1024, fill_x)
    begin(X, 1)
    for copy in loads[2:]:
        copy.start()
    loads[1].wait()

    def fill_d(at):
        buf_b[:, :, at] = (nn(sel[...], cot[:, at]) * row_gate).astype(BF16).reshape(n_exp, cap, at.size)

    half_chunks(0, 1024, fill_d)
    half_chunks(1, 1024, fill_d)
    begin(DY, 0, after=((X, 0), (X, 1)))

    finish(X, 0)
    finish(X, 1)
    part = model // (2 * SIDE)

    def x_part(zz, core):
        return pl.ds(pl.multiple_of((zz * 2 + core) * part, part), part)

    def to_sibling(src, dst, i):
        return pltpu.make_async_remote_copy(
            src_ref=src, dst_ref=dst, send_sem=sib_send.at[i], recv_sem=sib_recv.at[i],
            device_id=sibling, device_id_type=MESH,
        )

    sib_x = [to_sibling(xr.at[:, :, x_part(zz, 1 - c)], xs.at[zz], zz) for zz in range(SIDE)]
    for copy in sib_x:
        copy.start()
    loads[2].wait()
    loads[3].wait()

    def up_proj(_, at):
        full = xr[...].reshape(rows, model)
        hv = nn(full, wg[:, at])
        uv = nn(full, wu[:, at])
        h[:, at] = hv
        u[:, at] = uv
        act[:, at] = (hv * jax.nn.sigmoid(hv) * uv).astype(BF16)

    chunks(hidden, 256, up_proj)
    fslice = hidden // (2 * SIDE)
    for half in range(2):
        piece = act[:, half * SIDE * fslice : (half + 1) * SIDE * fslice].astype(F32).T.astype(BF16)
        for q in range(SIDE):
            index = half * SIDE + q
            act_t[index % 2, index // 2] = piece[q * fslice : (q + 1) * fslice, :]
    sib_act = to_sibling(act_t.at[1 - c], act_s, 4)
    sib_act.start()
    loads[4].wait()

    def down_proj(_, at):
        buf_a[:, :, at] = nn(act[...], wd[:, at]).astype(BF16).reshape(n_exp, cap, at.size)

    chunks(model, 1024, down_proj)
    begin(DY, 1, after=((DY, 0),))

    finish(DY, 0)

    def sib_d(half):
        return to_sibling(
            dd.at[pl.ds(0, n_exp), :, columns_of(half)], dd.at[pl.ds(n_exp, n_exp), :, columns_of(half)], 5 + half
        )

    sib_d(0).start()

    def back_act(half):
        def body(_, at):
            dact[:, at] = nt(dd[0:n_exp, :, half * width : (half + 1) * width].reshape(rows, width), wd[at, columns_of(half)])

        return body

    chunks(hidden, 256, back_act(0))

    def grad_down(at):
        left = jnp.concatenate([act_t[c].reshape(SIDE * fslice, rows), act_s[...].reshape(SIDE * fslice, rows)], axis=1)
        wd[0 : SIDE * fslice, at] = nn(left, dd[:, :, at].reshape(2 * rows, at.size)).astype(BF16)

    sib_act.wait()
    sib_d(0).wait()
    half_chunks(0, 512, grad_down)

    half_f, half_p = fslice // 2, part // 2

    def half_of(kind, zz, half):
        if kind in DOWN:
            return wd.at[pl.ds(pl.multiple_of(zz * fslice + half * half_f, half_f), half_f), columns_of(kind)]
        return (dwg, dwu)[kind - GATE].at[zz, pl.ds(half * half_p, half_p)]

    zr = (zr_d.at[0], zr_d.at[1], zr_g, zr_u)

    def hop(kind, i, src, device):
        return pltpu.make_async_remote_copy(
            src_ref=src, dst_ref=zr[kind].at[i], send_sem=z_send.at[kind, i], recv_sem=z_recv.at[kind, i],
            device_id=device, device_id_type=MESH,
        )

    def ring(kind, i):
        zz, half = ((z_far, 1), (z_far, 0), (z_up, 0), (z_down, 1), (z_up, 1), (z_down, 0))[i]
        return hop(kind, i, half_of(kind, zz, half), down if i % 2 else up)

    def first_hops(kind):
        for i in range(4):
            ring(kind, i).start()

    def relay(kind):
        for i, zz, half in ((0, z_up, 1), (1, z_down, 0)):
            ring(kind, i).wait_recv()
            mine = half_of(kind, zz, half)
            mine[...] = (mine[...].astype(F32) + zr[kind][i].astype(F32)).astype(BF16)
            ring(kind, i + 4).start()

    def total(kind, out):
        for i in (2, 3, 4, 5):
            ring(kind, i).wait_recv()
        for half, (a, b) in enumerate(((2, 5), (3, 4))):
            mine = half_of(kind, z, half)
            mine[...] = (mine[...].astype(F32) + zr[kind][a].astype(F32) + zr[kind][b].astype(F32)).astype(BF16)
        if kind in DOWN:
            whole = wd.at[pl.ds(pl.multiple_of(z * fslice, fslice), fslice), columns_of(kind)]
            out = out.at[0, :, columns_of(kind)]
        else:
            whole, out = (dwg, dwu)[kind - GATE].at[z], out.at[0]
        copy = pltpu.make_async_copy(whole, out, store.at[2 + kind])
        copy.start()
        return copy

    first_hops(DOWN[0])
    begin(OUT, 0, after=((DY, 1),))
    begin(OUT, 1)
    relay(DOWN[0])
    finish(DY, 1)
    sib_d(1).start()

    def back_act_last(_, at):
        da = dact[:, at] + nt(dd[0:n_exp, :, width:].reshape(rows, width), wd[at, columns_of(1)])
        hv, uv = h[:, at], u[:, at]
        sg = jax.nn.sigmoid(hv)
        dhc[0:rows, at] = (da * uv * sg * (1.0 + hv * (1.0 - sg))).astype(BF16)
        duc[0:rows, at] = (da * hv * sg).astype(BF16)

    chunks(hidden, 256, back_act_last)
    sib_dh = to_sibling(dhc.at[pl.ds(0, rows)], dhc.at[pl.ds(rows, rows)], 7)
    sib_du = to_sibling(duc.at[pl.ds(0, rows)], duc.at[pl.ds(rows, rows)], 8)
    sib_dh.start()
    sib_du.start()
    sib_d(1).wait()
    half_chunks(1, 512, grad_down)
    first_hops(DOWN[1])
    for copy in sib_x:
        copy.wait()

    def grad_in(right, out):
        @pl.loop(0, SIDE)
        def _(i):
            zz = (z + 2 + i) % SIDE
            left = jnp.concatenate([xr[:, :, x_part(zz, c)].reshape(rows, part), xs[zz].reshape(rows, part)], axis=0)
            out[zz] = tn(left, right[...]).astype(BF16)

    sib_dh.wait()
    grad_in(dhc, dwg)
    first_hops(GATE)
    sib_du.wait()
    grad_in(duc, dwu)
    first_hops(UP)
    for i in range(len(SHIFTS)):
        pl.semaphore_signal(credit, inc=1, device_id=(r, peer(SHIFTS[i])), device_id_type=MESH)

    def back_rows(_, at):
        buf_b[:, :, at] = (nt(dhc[0:rows], wg[at, :]) + nt(duc[0:rows], wu[at, :])).astype(BF16).reshape(n_exp, cap, at.size)

    chunks(model, 512, back_rows)
    relay(DOWN[1])
    pl.semaphore_wait(credit, len(SHIFTS))
    begin(DX, 0, after=((OUT, 0), (OUT, 1)))

    finish(OUT, 0)
    finish(OUT, 1)
    fetch = pltpu.make_async_copy(out_back, dd.at[pl.ds(n_exp, n_exp)], load.at[5])
    fetch.start()
    fetch.wait()
    gg[...] = jnp.zeros_like(gg)

    def combine(_, at):
        pairs = nn(sel_t[...], dd[n_exp : 2 * n_exp, :, at].reshape(rows, at.size))
        p0, p1 = pairs[0:toks], pairs[toks : 2 * toks]
        tok[:, at] = (gate0 * p0 + gate1 * p1).astype(BF16)
        cv = cot[:, at].astype(F32)
        for k, pk in enumerate((p0, p1)):
            prod = cv * pk
            for j in range(0, at.size, 128):
                gg[k] += prod[:, j : j + 128]

    chunks(model, 512, combine)
    mixed_out = pltpu.make_async_copy(tok, mixed, store.at[0])
    mixed_out.start()
    grad_gates[0:1, :] = jnp.sum(gg[0].T, axis=0, keepdims=True)
    grad_gates[1:2, :] = jnp.sum(gg[1].T, axis=0, keepdims=True)
    relay(GATE)
    begin(DX, 1, after=((DX, 0),))
    relay(UP)
    stores = [mixed_out] + [total(kind, grad_d) for kind in DOWN]

    def combine_dx(at):
        both = sel_t[0:toks, :] + sel_t[toks : 2 * toks, :]
        cot[:, at] = nn(both, xr[:, :, at].reshape(rows, at.size)).astype(BF16)

    finish(DX, 0)
    finish(DX, 1)
    chunks(model, 512, lambda _, at: combine_dx(at))
    stores.append(pltpu.make_async_copy(cot, grad_tok, store.at[1]))
    stores[-1].start()
    stores += [total(GATE, grad_g), total(UP, grad_u)]
    for i in range(len(SHIFTS)):
        block(DX, 1, i).wait_send()
    for kind in (*DOWN, GATE, UP):
        for i in range(6):
            ring(kind, i).wait_send()
    for copy in stores:
        copy.wait()


def copy_out(*refs):
    n = len(refs) // 3
    ins, outs, held, (load, store) = refs[:n], refs[n : 2 * n], refs[2 * n : 3 * n], refs[3 * n :]
    loads = [pltpu.make_async_copy(ins[i], held[i], load.at[i]) for i in range(n)]
    stores = [pltpu.make_async_copy(held[i], outs[i], store.at[i]) for i in range(n)]
    for copy in loads:
        copy.start()
    for first, second in zip(loads, stores):
        first.wait()
        second.start()
    for copy in stores:
        copy.wait()


def per_device(tokens, routes, gates, cotangent, w_gate, w_up, w_down):
    experts, replicas = lax.axis_size("expert"), lax.axis_size("dp")
    toks, model = tokens.shape
    hidden = w_gate.shape[2]
    cap = toks * routes.shape[1] * 3 // (2 * experts)
    rows = experts * cap
    part, fslice = model // replicas, hidden // replicas
    shape = jax.ShapeDtypeStruct
    any_space, vmem = pl.BlockSpec(memory_space=pl.ANY), pl.BlockSpec(memory_space=pltpu.VMEM)
    dma = pltpu.SemaphoreType.DMA
    n = len(SHIFTS)
    outs = pl.pallas_call(
        kernel,
        out_shape=(
            shape((toks, model), BF16),
            shape((toks, model), BF16),
            shape((2, toks), F32),
            shape((1, part, hidden), BF16),
            shape((1, part, hidden), BF16),
            shape((1, fslice, model), BF16),
            shape((experts, cap, model), BF16),
        ),
        in_specs=[vmem, vmem] + [any_space] * 5,
        out_specs=(any_space, any_space, vmem) + (any_space,) * 4,
        scratch_shapes=[
            pltpu.VMEM((toks, model), BF16),
            pltpu.VMEM((toks, model), BF16),
            pltpu.VMEM((model, hidden), BF16),
            pltpu.VMEM((model, hidden), BF16),
            pltpu.VMEM((hidden, model), BF16),
            pltpu.VMEM((rows, toks), BF16),
            pltpu.VMEM((2 * toks, rows), BF16),
            pltpu.VMEM((experts, cap, model), BF16),
            pltpu.VMEM((experts, cap, model), BF16),
            pltpu.VMEM((experts, cap, model), BF16),
            pltpu.VMEM((2 * experts, cap, model), BF16),
            pltpu.VMEM((SIDE, experts, cap, part), BF16),
            pltpu.VMEM((rows, hidden), F32),
            pltpu.VMEM((rows, hidden), F32),
            pltpu.VMEM((rows, hidden), BF16),
            pltpu.VMEM((2 * rows, hidden), BF16),
            pltpu.VMEM((2 * rows, hidden), BF16),
            pltpu.VMEM((2, SIDE, fslice, rows), BF16),
            pltpu.VMEM((SIDE, fslice, rows), BF16),
            pltpu.VMEM((SIDE, part, hidden), BF16),
            pltpu.VMEM((SIDE, part, hidden), BF16),
            pltpu.VMEM((6, part // 2, hidden), BF16),
            pltpu.VMEM((6, part // 2, hidden), BF16),
            pltpu.VMEM((2, 6, fslice // 2, model // 2), BF16),
            pltpu.VMEM((rows, hidden), F32),
            pltpu.VMEM((2, toks, 128), F32),
            dma((4, HALVES, n)),
            dma((4, HALVES, n)),
            dma((4, HALVES)),
            dma((9,)),
            dma((9,)),
            dma((4, 6)),
            dma((4, 6)),
            dma((6,)),
            dma((6,)),
            pltpu.SemaphoreType.REGULAR,
        ],
        compiler_params=pltpu.CompilerParams(
            collective_id=0, has_side_effects=True, vmem_limit_bytes=63 << 20
        ),
        name="expert_layer",
    )(routes.T, gates.T, tokens, cotangent, w_gate, w_up, w_down)
    outs = outs[:6]
    outs = pl.pallas_call(
        copy_out,
        out_shape=tuple(shape(o.shape, o.dtype) for o in outs),
        in_specs=[any_space] * len(outs),
        out_specs=(any_space,) * len(outs),
        scratch_shapes=[pltpu.VMEM(o.shape, o.dtype) for o in outs] + [dma((len(outs),))] * 2,
        compiler_params=pltpu.CompilerParams(vmem_limit_bytes=60 << 20),
        name="copy_out",
    )(*outs)
    return (outs[0], outs[1], outs[2].T, outs[3], outs[4], outs[5])


def solution(mesh):
    rows, whole = P(("dp", "expert"), None), P("expert", None, None)
    grads = P("expert", "dp", None)
    return jax.shard_map(
        per_device,
        mesh=mesh,
        in_specs=(rows,) * 4 + (whole,) * 3,
        out_specs=(rows,) * 3 + (grads,) * 3,
        check_vma=False,
    )
```

```python
import jax
import jax.numpy as jnp
from jax import lax
from jax.experimental import pallas as pl
from jax.experimental.pallas import tpu as pltpu
from jax.sharding import PartitionSpec as P

MESH = pl.DeviceIdType.MESH
F32, BF16 = jnp.float32, jnp.bfloat16
SIDE = 4
GROUPS = (
    ((1, 3), (3, 1)),
    ((1, 1), (3, 3)),
    ((0, 2), (2, 0)),
    ((2, 2),),
    ((1, 2), (3, 2), (1, 0), (3, 0)),
    ((2, 1), (2, 3), (0, 1), (0, 3)),
)
SHIFTS = tuple(shift for group in GROUPS for shift in group)
X, DY, OUT, DX = range(4)
PARTS = (2, 4, 2, 2)
DOWN, GATE, UP = (0, 1, 2, 3), 4, 5


def nn(a, b):
    return lax.dot_general(a, b, (((1,), (0,)), ((), ())), preferred_element_type=F32)


def nt(a, b):
    return lax.dot_general(a, b, (((1,), (1,)), ((), ())), preferred_element_type=F32)


def tn(a, b):
    return lax.dot_general(a, b, (((0,), (0,)), ((), ())), preferred_element_type=F32)


def kernel(
    routes, gates, tok_in, cot_in, wg_in, wu_in, wd_in,
    mixed, grad_tok, grad_gates, grad_g, grad_u, grad_d, out_back,
    tok, cot, wg, wu, wd, sel, sel_t, buf_a, buf_b, xr, dd, xs, h, u, act, dhc, duc, act_t, act_s, dwg, dwu,
    zr_g, zr_u, zr_d, dact, gg,
    send, recv, local, sib_send, sib_recv, z_send, z_recv, load, store, credit,
):
    n_exp, cap, model = buf_a.shape
    rows = n_exp * cap
    hidden = act.shape[1]
    toks = tok.shape[0]
    r, e = lax.axis_index("dp"), lax.axis_index("expert")
    z, c = r // 2, r % 2
    y, x = e // SIDE, e % SIDE

    def peer(shift, sign=1):
        dy, dx = shift
        return (y + sign * dy + SIDE) % SIDE * SIDE + (x + sign * dx + SIDE) % SIDE

    sibling = (r + 1 - 2 * c, e)
    z_up, z_down, z_far = (z + 1) % SIDE, (z + 3) % SIDE, (z + 2) % SIDE
    up, down = (z_up * 2 + c, e), (z_down * 2 + c, e)

    loads = [
        pltpu.make_async_copy(src, dst, load.at[i])
        for i, (src, dst) in enumerate(((tok_in, tok), (cot_in, cot), (wg_in.at[0], wg), (wu_in.at[0], wu), (wd_in.at[0], wd)))
    ]
    for copy in loads[:2]:
        copy.start()
    barrier = pltpu.get_barrier_semaphore()
    for shift in SHIFTS:
        pl.semaphore_signal(barrier, inc=1, device_id=(r, peer(shift)), device_id_type=MESH)
    for device in (sibling, up, down):
        pl.semaphore_signal(barrier, inc=1, device_id=device, device_id_type=MESH)

    r0, r1 = routes[0:1, :], routes[1:2, :]
    g0, g1 = gates[0:1, :], gates[1:2, :]
    expert_id = lax.broadcasted_iota(jnp.int32, (n_exp, toks), 0)
    on0, on1 = expert_id == r0, expert_id == r1
    named = jnp.where(on0 | on1, 1.0, 0.0).astype(BF16)
    before = lax.broadcasted_iota(jnp.int32, (toks, toks), 0) < lax.broadcasted_iota(jnp.int32, (toks, toks), 1)
    place = nn(named, jnp.where(before, 1.0, 0.0).astype(BF16))
    s0 = jnp.sum(jnp.where(on0, place, 0.0), axis=0, keepdims=True) + (r0 * cap).astype(F32)
    s1 = jnp.sum(jnp.where(on1, place, 0.0), axis=0, keepdims=True) + (r1 * cap).astype(F32)
    slot = lax.broadcasted_iota(jnp.int32, (rows, toks), 0).astype(F32)
    hit0, hit1 = slot == s0, slot == s1
    sel[...] = jnp.where(hit0 | hit1, 1.0, 0.0).astype(BF16)
    row_gate = jnp.sum(jnp.where(hit0, g0, 0.0) + jnp.where(hit1, g1, 0.0), axis=1, keepdims=True)
    line = lax.broadcasted_iota(jnp.int32, (toks, toks), 0)
    columns = jnp.where(line == 0, s0, jnp.where(line == 1, s1, jnp.where(line == 2, g0, g1))).T
    slot_t = lax.broadcasted_iota(jnp.int32, (toks, rows), 1).astype(F32)
    sel_t[0:toks, :] = jnp.where(slot_t == columns[:, 0:1], 1.0, 0.0).astype(BF16)
    sel_t[toks : 2 * toks, :] = jnp.where(slot_t == columns[:, 1:2], 1.0, 0.0).astype(BF16)
    gate0, gate1 = columns[:, 2:3], columns[:, 3:4]

    def chunks(total, size, body):
        @pl.loop(0, total // size)
        def _(i):
            body(i, pl.ds(pl.multiple_of(i * size, size), size))

    source = (buf_a, buf_b, buf_a, buf_b)
    target = (xr, dd, out_back, xr)

    def columns_of(kind, half):
        width = model // PARTS[kind]
        return pl.ds(half * width, width)

    def block(kind, half, i):
        to = peer(SHIFTS[i])
        return pltpu.make_async_remote_copy(
            src_ref=source[kind].at[to, :, columns_of(kind, half)], dst_ref=target[kind].at[e, :, columns_of(kind, half)],
            send_sem=send.at[kind, half, i], recv_sem=recv.at[kind, half, i],
            device_id=(r, to), device_id_type=MESH,
        )

    def arriving(kind, half, i):
        return pltpu.make_async_remote_copy(
            src_ref=source[kind].at[e, :, columns_of(kind, half)],
            dst_ref=target[kind].at[peer(SHIFTS[i], -1), :, columns_of(kind, half)],
            send_sem=send.at[kind, half, i], recv_sem=recv.at[kind, half, i],
            device_id=(r, peer(SHIFTS[i])), device_id_type=MESH,
        )

    def own(kind, half):
        return pltpu.make_async_copy(
            source[kind].at[e, :, columns_of(kind, half)], target[kind].at[e, :, columns_of(kind, half)], local.at[kind, half]
        )

    def begin(kind, half, after=(), groups=range(len(GROUPS))):
        if 0 in groups:
            own(kind, half).start()
        for g in groups:
            group = GROUPS[g]
            first = sum(len(x) for x in GROUPS[:g])
            for i in range(first, first + len(group)):
                for earlier in after:
                    block(*earlier, i).wait_send()
            for i in range(first, first + len(group)):
                block(kind, half, i).start()

    def finish(kind, half):
        own(kind, half).wait()
        for i in range(len(SHIFTS)):
            arriving(kind, half, i).wait_recv()

    def part_chunks(kind, half, size, body):
        width = model // PARTS[kind]

        @pl.loop(0, width // size)
        def _(i):
            body(pl.ds(pl.multiple_of(half * width + i * size, size), size))

    loads[0].wait()

    def fill_x(at):
        buf_a[:, :, at] = nn(sel[...], tok[:, at]).astype(BF16).reshape(n_exp, cap, at.size)

    part_chunks(X, 0, 1024, fill_x)
    pl.semaphore_wait(barrier, len(SHIFTS) + 3)
    begin(X, 0)
    part_chunks(X, 1, 1024, fill_x)
    begin(X, 1)
    for copy in loads[2:]:
        copy.start()
    loads[1].wait()

    def fill_d(at):
        buf_b[:, :, at] = (nn(sel[...], cot[:, at]) * row_gate).astype(BF16).reshape(n_exp, cap, at.size)

    chunks(model, 1024, lambda _, at: fill_d(at))
    begin(DY, 0, after=((X, 0), (X, 1)))
    begin(DY, 1)

    finish(X, 0)
    finish(X, 1)
    part = model // (2 * SIDE)

    def x_part(zz, core):
        return pl.ds(pl.multiple_of((zz * 2 + core) * part, part), part)

    def to_sibling(src, dst, i):
        return pltpu.make_async_remote_copy(
            src_ref=src, dst_ref=dst, send_sem=sib_send.at[i], recv_sem=sib_recv.at[i],
            device_id=sibling, device_id_type=MESH,
        )

    sib_x = [to_sibling(xr.at[:, :, x_part(zz, 1 - c)], xs.at[zz], zz) for zz in range(SIDE)]
    for copy in sib_x:
        copy.start()
    loads[2].wait()
    loads[3].wait()

    def up_proj(_, at):
        full = xr[...].reshape(rows, model)
        hv = nn(full, wg[:, at])
        uv = nn(full, wu[:, at])
        h[:, at] = hv
        u[:, at] = uv
        act[:, at] = (hv * jax.nn.sigmoid(hv) * uv).astype(BF16)

    chunks(hidden, 256, up_proj)
    begin(DY, 2, after=((DY, 0),))
    fslice = hidden // (2 * SIDE)
    for half in range(2):
        piece = act[:, half * SIDE * fslice : (half + 1) * SIDE * fslice].astype(F32).T.astype(BF16)
        for q in range(SIDE):
            index = half * SIDE + q
            act_t[index % 2, index // 2] = piece[q * fslice : (q + 1) * fslice, :]
    sib_act = to_sibling(act_t.at[1 - c], act_s, 4)
    sib_act.start()
    loads[4].wait()

    def down_proj(_, at):
        buf_a[:, :, at] = nn(act[...], wd[:, at]).astype(BF16).reshape(n_exp, cap, at.size)

    chunks(model, 1024, down_proj)

    half_f, half_p = fslice // 2, part // 2

    def half_of(kind, zz, half):
        if kind in DOWN:
            return wd.at[pl.ds(pl.multiple_of(zz * fslice + half * half_f, half_f), half_f), columns_of(DY, kind)]
        return (dwg, dwu)[kind - GATE].at[zz, pl.ds(half * half_p, half_p)]

    zr = (*(zr_d.at[i] for i in DOWN), zr_g, zr_u)

    def hop(kind, i, src, device):
        return pltpu.make_async_remote_copy(
            src_ref=src, dst_ref=zr[kind].at[i], send_sem=z_send.at[kind, i], recv_sem=z_recv.at[kind, i],
            device_id=device, device_id_type=MESH,
        )

    def ring(kind, i):
        zz, half = ((z_far, 1), (z_far, 0), (z_up, 0), (z_down, 1), (z_up, 1), (z_down, 0))[i]
        return hop(kind, i, half_of(kind, zz, half), down if i % 2 else up)

    def first_hops(kind):
        for i in range(4):
            ring(kind, i).start()

    def relay(kind):
        for i, zz, half in ((0, z_up, 1), (1, z_down, 0)):
            ring(kind, i).wait_recv()
            mine = half_of(kind, zz, half)
            mine[...] = (mine[...].astype(F32) + zr[kind][i].astype(F32)).astype(BF16)
            ring(kind, i + 4).start()

    def total(kind, out):
        for i in (2, 3, 4, 5):
            ring(kind, i).wait_recv()
        for half, (a, b) in enumerate(((2, 5), (3, 4))):
            mine = half_of(kind, z, half)
            mine[...] = (mine[...].astype(F32) + zr[kind][a].astype(F32) + zr[kind][b].astype(F32)).astype(BF16)
        if kind in DOWN:
            whole = wd.at[pl.ds(pl.multiple_of(z * fslice, fslice), fslice), columns_of(DY, kind)]
            out = out.at[0, :, columns_of(DY, kind)]
        else:
            whole, out = (dwg, dwu)[kind - GATE].at[z], out.at[0]
        copy = pltpu.make_async_copy(whole, out, store.at[2 + kind])
        copy.start()
        return copy

    def sib_d(half):
        at = columns_of(DY, half)
        return to_sibling(dd.at[pl.ds(0, n_exp), :, at], dd.at[pl.ds(n_exp, n_exp), :, at], 5 + half)

    def back_act(half):
        at = columns_of(DY, half)
        return lambda f: nt(dd[0:n_exp, :, at].reshape(rows, at.size), wd[f, at])

    def grad_down(at):
        left = jnp.concatenate([act_t[c].reshape(SIDE * fslice, rows), act_s[...].reshape(SIDE * fslice, rows)], axis=1)
        wd[0 : SIDE * fslice, at] = nn(left, dd[:, :, at].reshape(2 * rows, at.size)).astype(BF16)

    last = PARTS[DY] - 1
    sib_act.wait()
    for half in range(last):
        finish(DY, half)
        sib_d(half).start()
        term = back_act(half)

        def add_act(_, f, half=half, term=term):
            dact[:, f] = term(f) if half == 0 else dact[:, f] + term(f)

        chunks(hidden, 256, add_act)
        sib_d(half).wait()
        part_chunks(DY, half, 512, grad_down)
        first_hops(DOWN[half])
        if half + 3 <= last:
            begin(DY, half + 3, after=((DY, half + 1),))
        else:
            begin(OUT, half + 3 - PARTS[DY], after=((DY, half + 1),))
        if half > 0:
            relay(DOWN[half - 1])
    finish(DY, last)
    sib_d(last).start()

    def back_act_last(_, at):
        da = dact[:, at] + back_act(last)(at)
        hv, uv = h[:, at], u[:, at]
        sg = jax.nn.sigmoid(hv)
        dhc[0:rows, at] = (da * uv * sg * (1.0 + hv * (1.0 - sg))).astype(BF16)
        duc[0:rows, at] = (da * hv * sg).astype(BF16)

    chunks(hidden, 256, back_act_last)
    sib_dh = to_sibling(dhc.at[pl.ds(0, rows)], dhc.at[pl.ds(rows, rows)], 9)
    sib_du = to_sibling(duc.at[pl.ds(0, rows)], duc.at[pl.ds(rows, rows)], 10)
    sib_dh.start()
    sib_du.start()
    sib_d(last).wait()
    part_chunks(DY, last, 512, grad_down)
    first_hops(DOWN[last])
    relay(DOWN[last - 1])
    for copy in sib_x:
        copy.wait()

    def grad_in(right, out):
        @pl.loop(0, SIDE)
        def _(i):
            zz = (z + 2 + i) % SIDE
            left = jnp.concatenate([xr[:, :, x_part(zz, c)].reshape(rows, part), xs[zz].reshape(rows, part)], axis=0)
            out[zz] = tn(left, right[...]).astype(BF16)

    sib_dh.wait()
    grad_in(dhc, dwg)
    first_hops(GATE)
    sib_du.wait()
    grad_in(duc, dwu)
    first_hops(UP)
    for i in range(len(SHIFTS)):
        pl.semaphore_signal(credit, inc=1, device_id=(r, peer(SHIFTS[i])), device_id_type=MESH)

    def back_rows(_, at):
        buf_b[:, :, at] = (nt(dhc[0:rows], wg[at, :]) + nt(duc[0:rows], wu[at, :])).astype(BF16).reshape(n_exp, cap, at.size)

    chunks(model, 512, back_rows)
    relay(DOWN[last])
    pl.semaphore_wait(credit, len(SHIFTS))
    begin(DX, 0, after=((OUT, 0), (OUT, 1)))

    finish(OUT, 0)
    finish(OUT, 1)
    fetch = pltpu.make_async_copy(out_back, dd.at[pl.ds(n_exp, n_exp)], load.at[5])
    fetch.start()
    fetch.wait()
    gg[...] = jnp.zeros_like(gg)

    def combine(_, at):
        pairs = nn(sel_t[...], dd[n_exp : 2 * n_exp, :, at].reshape(rows, at.size))
        p0, p1 = pairs[0:toks], pairs[toks : 2 * toks]
        tok[:, at] = (gate0 * p0 + gate1 * p1).astype(BF16)
        cv = cot[:, at].astype(F32)
        for k, pk in enumerate((p0, p1)):
            prod = cv * pk
            for j in range(0, at.size, 128):
                gg[k] += prod[:, j : j + 128]

    chunks(model, 512, combine)
    mixed_out = pltpu.make_async_copy(tok, mixed, store.at[0])
    mixed_out.start()
    grad_gates[0:1, :] = jnp.sum(gg[0].T, axis=0, keepdims=True)
    grad_gates[1:2, :] = jnp.sum(gg[1].T, axis=0, keepdims=True)
    relay(GATE)
    begin(DX, 1, after=((DX, 0),))
    relay(UP)
    stores = [mixed_out] + [total(kind, grad_d) for kind in DOWN]

    def combine_dx(at):
        both = sel_t[0:toks, :] + sel_t[toks : 2 * toks, :]
        cot[:, at] = nn(both, xr[:, :, at].reshape(rows, at.size)).astype(BF16)

    finish(DX, 0)
    part_chunks(DX, 0, 512, combine_dx)
    finish(DX, 1)
    part_chunks(DX, 1, 512, combine_dx)
    stores.append(pltpu.make_async_copy(cot, grad_tok, store.at[1]))
    stores[-1].start()
    stores += [total(GATE, grad_g), total(UP, grad_u)]
    for i in range(len(SHIFTS)):
        block(DX, 1, i).wait_send()
    for kind in (*DOWN, GATE, UP):
        for i in range(6):
            ring(kind, i).wait_send()
    for copy in stores:
        copy.wait()


def copy_out(*refs):
    n = len(refs) // 3
    ins, outs, held, (load, store) = refs[:n], refs[n : 2 * n], refs[2 * n : 3 * n], refs[3 * n :]
    loads = [pltpu.make_async_copy(ins[i], held[i], load.at[i]) for i in range(n)]
    stores = [pltpu.make_async_copy(held[i], outs[i], store.at[i]) for i in range(n)]
    for copy in loads:
        copy.start()
    for first, second in zip(loads, stores):
        first.wait()
        second.start()
    for copy in stores:
        copy.wait()


def per_device(tokens, routes, gates, cotangent, w_gate, w_up, w_down):
    experts, replicas = lax.axis_size("expert"), lax.axis_size("dp")
    toks, model = tokens.shape
    hidden = w_gate.shape[2]
    cap = toks * routes.shape[1] * 3 // (2 * experts)
    rows = experts * cap
    part, fslice = model // replicas, hidden // replicas
    shape = jax.ShapeDtypeStruct
    any_space, vmem = pl.BlockSpec(memory_space=pl.ANY), pl.BlockSpec(memory_space=pltpu.VMEM)
    dma = pltpu.SemaphoreType.DMA
    n = len(SHIFTS)
    outs = pl.pallas_call(
        kernel,
        out_shape=(
            shape((toks, model), BF16),
            shape((toks, model), BF16),
            shape((2, toks), F32),
            shape((1, part, hidden), BF16),
            shape((1, part, hidden), BF16),
            shape((1, fslice, model), BF16),
            shape((experts, cap, model), BF16),
        ),
        in_specs=[vmem, vmem] + [any_space] * 5,
        out_specs=(any_space, any_space, vmem) + (any_space,) * 4,
        scratch_shapes=[
            pltpu.VMEM((toks, model), BF16),
            pltpu.VMEM((toks, model), BF16),
            pltpu.VMEM((model, hidden), BF16),
            pltpu.VMEM((model, hidden), BF16),
            pltpu.VMEM((hidden, model), BF16),
            pltpu.VMEM((rows, toks), BF16),
            pltpu.VMEM((2 * toks, rows), BF16),
            pltpu.VMEM((experts, cap, model), BF16),
            pltpu.VMEM((experts, cap, model), BF16),
            pltpu.VMEM((experts, cap, model), BF16),
            pltpu.VMEM((2 * experts, cap, model), BF16),
            pltpu.VMEM((SIDE, experts, cap, part), BF16),
            pltpu.VMEM((rows, hidden), F32),
            pltpu.VMEM((rows, hidden), F32),
            pltpu.VMEM((rows, hidden), BF16),
            pltpu.VMEM((2 * rows, hidden), BF16),
            pltpu.VMEM((2 * rows, hidden), BF16),
            pltpu.VMEM((2, SIDE, fslice, rows), BF16),
            pltpu.VMEM((SIDE, fslice, rows), BF16),
            pltpu.VMEM((SIDE, part, hidden), BF16),
            pltpu.VMEM((SIDE, part, hidden), BF16),
            pltpu.VMEM((6, part // 2, hidden), BF16),
            pltpu.VMEM((6, part // 2, hidden), BF16),
            pltpu.VMEM((PARTS[DY], 6, fslice // 2, model // PARTS[DY]), BF16),
            pltpu.VMEM((rows, hidden), F32),
            pltpu.VMEM((2, toks, 128), F32),
            dma((4, max(PARTS), n)),
            dma((4, max(PARTS), n)),
            dma((4, max(PARTS))),
            dma((11,)),
            dma((11,)),
            dma((6, 6)),
            dma((6, 6)),
            dma((6,)),
            dma((8,)),
            pltpu.SemaphoreType.REGULAR,
        ],
        compiler_params=pltpu.CompilerParams(
            collective_id=0, has_side_effects=True, vmem_limit_bytes=63 << 20
        ),
        name="expert_layer",
    )(routes.T, gates.T, tokens, cotangent, w_gate, w_up, w_down)
    outs = outs[:6]
    outs = pl.pallas_call(
        copy_out,
        out_shape=tuple(shape(o.shape, o.dtype) for o in outs),
        in_specs=[any_space] * len(outs),
        out_specs=(any_space,) * len(outs),
        scratch_shapes=[pltpu.VMEM(o.shape, o.dtype) for o in outs] + [dma((len(outs),))] * 2,
        compiler_params=pltpu.CompilerParams(vmem_limit_bytes=60 << 20),
        name="copy_out",
    )(*outs)
    return (outs[0], outs[1], outs[2].T, outs[3], outs[4], outs[5])


def solution(mesh):
    rows, whole = P(("dp", "expert"), None), P("expert", None, None)
    grads = P("expert", "dp", None)
    return jax.shard_map(
        per_device,
        mesh=mesh,
        in_specs=(rows,) * 4 + (whole,) * 3,
        out_specs=(rows,) * 3 + (grads,) * 3,
        check_vma=False,
    )
```
